128 devices in a mesh: dp: 64 (over x, y, z_lo, core), tensor: 2 (over z_hi).
Axes of the slice: x: 4, y: 4, z: 4 (z_hi: 2, z_lo: 2; z = z_hi * 2 + z_lo), core: 2. Of those that a mesh axis runs over, the one named last changes fastest.
Arguments:
- frames: bfloat16 [64, 1500, 1280], P('dp', 'tensor'), may hold values from -6 to 6
- frame_counts: int32 [64], P('dp'), may hold values from 2 to 1500
- encoder_gain: float32 [1280], replicated, may hold values from 0.25 to 1.75
- encoder_shift: float32 [1280], replicated, may hold values from -3 to 3
- encoder_qkv: bfloat16 [3, 1280, 640], P(None, 'dp', 'tensor'), may hold values from -0.25 to 0.25
- encoder_out: bfloat16 [640, 1280], P('tensor', 'dp'), may hold values from -0.25 to 0.25
- post_gain: float32 [1280], replicated, may hold values from 0.25 to 1.75
- post_shift: float32 [1280], replicated, may hold values from -3 to 3
- projector: bfloat16 [1280, 2048], P('dp', 'tensor'), may hold values from -0.15625 to 0.15625
- projector_shift: float32 [2048], replicated, may hold values from -3 to 3
- text_embed: bfloat16 [64, 42, 2048], P('dp', 'tensor'), may hold values from -6 to 6
- decoder_gain: float32 [2048], replicated, may hold values from 0.25 to 1.75
- decoder_qkv: bfloat16 [3, 2048, 2048], P(None, 'dp', 'tensor'), may hold values from -0.25 to 0.25
- adapter_in: float32 [2, 2048, 64], replicated, may hold values from -0.125 to 0.125
- adapter_out: float32 [2, 64, 2048], P(None, None, 'tensor'), may hold values from -0.75 to 0.75
- audio_upstream: bfloat16 [64, 750, 2048], P('dp', None, 'tensor'), may hold values from -0.29882812 to 0.29882812
- text_upstream: bfloat16 [64, 42, 2048], P('dp', None, 'tensor'), may hold values from -0.29882812 to 0.29882812
Outputs:
- adapter_in_grad: float32 [2, 2048, 64], P(None, ('dp', 'tensor'))
- adapter_out_grad: float32 [2, 64, 2048], P(None, 'dp', 'tensor')
The draws below stay inside these ranges and needn't reach their ends.
All inputs are finite; a program needn't handle non-finite values.
Results may differ from the reference program's by a relative error of at most 0.034.
Values may be sent and summed in bfloat16 or wider, within the bound.
No kernel may reach another device: no remote copies, remote signals or barrier semaphores. Data moves between devices by JAX's collectives and lax.ppermute only.
A program may use at most 128 MiB of HBM per device.

```python
import jax
import jax.numpy as jnp
from jax import lax

DE = 1280
EHD = 64
FRAMES = 1500
D = 2048
HD = 128
RANK = 64
TEXT = 42
EW = 640
HQ = 2048
AUDIO = 750
CLIPS = 64


def draw_frames(key, part):
    key = jax.random.fold_in(key, 1)
    noise_part = jax.random.normal(key, (CLIPS, FRAMES, DE), jnp.float32)
    result_rows = noise_part
    return jnp.clip(result_rows, -6.0, 6.0).astype(jnp.bfloat16)


def draw_text_embed(key, part):
    key = jax.random.fold_in(key, 3)
    noise_part = jax.random.normal(key, (CLIPS, TEXT, D), jnp.float32)
    result_rows = noise_part
    return jnp.clip(result_rows, -6.0, 6.0).astype(jnp.bfloat16)


def draw_encoder_qkv(key, part):
    key = jax.random.fold_in(key, 2)
    entries = jnp.clip(jax.random.normal(key, (3, DE, EW), jnp.float32), -6.0, 6.0) * DE ** (-0.5)
    return jnp.clip(entries, -0.25, 0.25).astype(jnp.bfloat16)


def draw_decoder_qkv(key, part):
    key = jax.random.fold_in(key, 4)
    entries = jnp.clip(jax.random.normal(key, (3, D, HQ), jnp.float32), -6.0, 6.0) * D ** (-0.5)
    return jnp.clip(entries, -0.25, 0.25).astype(jnp.bfloat16)


def touch_ends(values, key, least, largest):
    extent = values.shape
    spot = [jax.random.randint(jax.random.fold_in(key, axis), (), 0, extent[axis]) for axis in range(len(extent))]
    values = values.at[tuple(spot)].set(least)
    longest = extent.index(max(extent))
    spot[longest] = (spot[longest] + 1) % extent[longest]
    return values.at[tuple(spot)].set(largest)


def block_levels(key, dims, pieces, least, top_value):
    def one(axis_at, blocks):
        draws = jax.random.uniform(jax.random.fold_in(jax.random.fold_in(key, 6), axis_at), (blocks,), jnp.float32, least / len(pieces), top_value / len(pieces))
        return jnp.repeat(jnp.exp(draws), dims[axis_at] // blocks).reshape((-1,) + (1,) * (len(dims) - axis_at - 1))

    level = one(*pieces[0])
    for cut in pieces[1:]:
        level = level * one(*cut)
    return level


def noise(stream_key, dims, scale, bound, split=(), kind=jnp.bfloat16):
    level = block_levels(stream_key, dims, split, -0.22, 0.18) if split else 1.0
    result = jax.random.normal(stream_key, dims, jnp.float32) * scale * level
    return jnp.minimum(jnp.maximum(result, -bound), bound).astype(kind)


def setup_inputs(seed: int = 0) -> dict:
    keys = jax.random.split(jax.random.key(seed), 18)
    frames = draw_frames(jax.random.fold_in(keys[17], 71), 0)
    frame_counts = touch_ends(jax.random.randint(keys[1], (CLIPS,), 2, FRAMES + 1), jax.random.fold_in(keys[1], 1), 2, FRAMES).astype(jnp.int32)
    encoder_gain = jnp.clip(1.0 + 0.15 * jax.random.normal(keys[2], (DE,), jnp.float32), 0.25, 1.75)
    encoder_shift = noise(keys[3], (DE,), 0.5, 3.0, (), jnp.float32)
    encoder_qkv = draw_encoder_qkv(jax.random.fold_in(keys[17], 71), 0)
    encoder_out = noise(keys[5], (EW, DE), EW ** -0.5, 0.25, ((0, 2), (1, 64)))
    post_gain = jnp.clip(1.0 + 0.15 * jax.random.normal(keys[6], (DE,), jnp.float32), 0.25, 1.75)
    post_shift = noise(keys[7], (DE,), 0.5, 3.0, (), jnp.float32)
    projector = noise(keys[8], (DE, D), DE ** -0.5, 0.15625, ((0, 64), (1, 2)))
    projector_shift = noise(keys[9], (D,), 0.5, 3.0, (), jnp.float32)
    text_embed = draw_text_embed(jax.random.fold_in(keys[17], 71), 0)
    decoder_gain = jnp.clip(1.0 + 0.15 * jax.random.normal(keys[11], (D,), jnp.float32), 0.25, 1.75)
    decoder_qkv = draw_decoder_qkv(jax.random.fold_in(keys[17], 71), 0)
    adapter_in = noise(keys[13], (2, D, RANK), D ** -0.5, 0.125, (), jnp.float32)
    adapter_out = noise(keys[14], (2, RANK, HQ), RANK ** -0.5, 0.75, ((2, 2),), jnp.float32)
    audio_upstream = noise(keys[15], (CLIPS, AUDIO, HQ), 0.05, 0.29882812, ((0, 64), (2, 2)))
    text_upstream = noise(keys[16], (CLIPS, TEXT, HQ), 0.05, 0.29882812, ((0, 64), (2, 2)))
    return {"frames": frames, "frame_counts": frame_counts, "encoder_gain": encoder_gain, "encoder_shift": encoder_shift, "encoder_qkv": encoder_qkv, "encoder_out": encoder_out, "post_gain": post_gain, "post_shift": post_shift, "projector": projector, "projector_shift": projector_shift, "text_embed": text_embed, "decoder_gain": decoder_gain, "decoder_qkv": decoder_qkv, "adapter_in": adapter_in, "adapter_out": adapter_out, "audio_upstream": audio_upstream, "text_upstream": text_upstream}


EPS_LAYER = 1e-05
EPS_ROOT = 1e-06
ADAPTER_SCALE = 2.0
ROPE_BASE = 10000.0
HIGHEST = lax.Precision.HIGHEST

def layer_norm(values, gain, shift):
    values = values.astype(jnp.float32)
    center = values - lax.optimization_barrier(jnp.mean(values, -1, keepdims=True))
    spread = lax.optimization_barrier(jnp.mean(center * center, -1, keepdims=True))
    return center * lax.rsqrt(spread + EPS_LAYER) * gain + shift

def root_norm(values, gain):
    values = values.astype(jnp.float32)
    return (values * lax.rsqrt(lax.optimization_barrier(jnp.mean(values * values, -1, keepdims=True)) + EPS_ROOT) * gain).astype(jnp.bfloat16)

def encoder_head(queries, keys_in, values_in, usable):
    scores = jnp.dot(queries, keys_in.T, preferred_element_type=jnp.float32) * queries.shape[-1] ** (-0.5)
    scores = jnp.where(usable[None, :], scores, -jnp.inf)
    row_top = lax.optimization_barrier(jnp.max(scores, -1, keepdims=True))
    weights = jnp.exp(scores - row_top)
    probabilities = (weights / lax.optimization_barrier(jnp.sum(weights, -1, keepdims=True))).astype(jnp.bfloat16)
    return jnp.dot(probabilities, values_in, preferred_element_type=jnp.float32).astype(jnp.bfloat16)

def encoder_attention(queries, keys_in, values_in, usable, head_width):
    length = queries.shape[0]

    def heads_first(array_in):
        return array_in.reshape(array_in.shape[0], -1, head_width).transpose(1, 0, 2)
    context = lax.map(lambda members: encoder_head(members[0], members[1], members[2], usable), (heads_first(queries), heads_first(keys_in), heads_first(values_in)))
    return context.transpose(1, 0, 2).reshape(length, -1)

def rope_tables(length, head_width):
    position = jnp.arange(length).astype(jnp.float32)
    frequency = ROPE_BASE ** (-jnp.arange(0, head_width, 2).astype(jnp.float32) / head_width)
    angles = position[:, None] * frequency[None, :]
    angles = jnp.concatenate([angles, angles], -1)
    return (jnp.cos(angles)[:, None, :], jnp.sin(angles)[:, None, :])

def rotate(values, cosine, sine_table):
    half_width = values.shape[-1] // 2
    turned = jnp.concatenate([-values[..., half_width:], values[..., :half_width]], -1)
    return values * cosine + turned * sine_table

def unrotate(grad_rows, cosine, sine_table):
    half_width = grad_rows.shape[-1] // 2
    scaled = grad_rows * sine_table
    back_part = jnp.concatenate([scaled[..., half_width:], -scaled[..., :half_width]], -1)
    return grad_rows * cosine + back_part

def decoder_head(queries, keys_in, values_in, upstream, allowed):
    score_scale = queries.shape[-1] ** (-0.5)
    scores = jnp.dot(queries, keys_in.T, preferred_element_type=jnp.float32) * score_scale
    scores = jnp.where(allowed, scores, -jnp.inf)
    row_top = lax.optimization_barrier(jnp.max(scores, -1, keepdims=True))
    weights = jnp.exp(scores - row_top)
    probabilities = weights / lax.optimization_barrier(jnp.sum(weights, -1, keepdims=True))
    rounded = probabilities.astype(jnp.bfloat16)
    context = jnp.dot(rounded, values_in, preferred_element_type=jnp.float32).astype(jnp.bfloat16)
    row_delta = lax.optimization_barrier(jnp.sum(upstream.astype(jnp.float32) * context.astype(jnp.float32), -1, keepdims=True))
    grad_probs = jnp.dot(upstream, values_in.T, preferred_element_type=jnp.float32)
    grad_scores = (probabilities * (grad_probs - row_delta) * score_scale).astype(jnp.bfloat16)
    grad_query = jnp.dot(grad_scores, keys_in, preferred_element_type=jnp.float32)
    grad_value = jnp.dot(rounded.T, upstream, preferred_element_type=jnp.float32)
    return (grad_query, grad_value)

def adapter_grads(normed, query_base, key_base, value_base, upstream, frame_count, audio_total, adapter_in, adapter_out, head_width):
    length = normed.shape[0]
    full_rows = normed.astype(jnp.float32)
    low_query = jnp.dot(full_rows, adapter_in[0], precision=HIGHEST)
    low_value = jnp.dot(full_rows, adapter_in[1], precision=HIGHEST)
    queries = query_base + ADAPTER_SCALE * jnp.dot(low_query, adapter_out[0], precision=HIGHEST)
    values_in = value_base + ADAPTER_SCALE * jnp.dot(low_value, adapter_out[1], precision=HIGHEST)
    cosine, sine_table = rope_tables(length, head_width)
    queries = rotate(queries.reshape(length, -1, head_width), cosine, sine_table).astype(jnp.bfloat16)
    keys_in = rotate(key_base.reshape(length, -1, head_width), cosine, sine_table).astype(jnp.bfloat16)
    values_in = values_in.reshape(length, -1, head_width).astype(jnp.bfloat16)
    upstream = upstream.reshape(length, -1, head_width)
    position = jnp.arange(length, dtype=jnp.int32)
    key_usable = (position >= audio_total) | (position < (frame_count + 1) // 2)
    allowed = (position[None, :] <= position[:, None]) & key_usable[None, :]

    def heads_first(array_in):
        return array_in.transpose(1, 0, 2)
    grad_query, grad_value = lax.map(lambda members: decoder_head(members[0], members[1], members[2], members[3], allowed), (heads_first(queries), heads_first(keys_in), heads_first(values_in), heads_first(upstream)))
    grad_query = unrotate(heads_first(grad_query), cosine, sine_table).reshape(length, -1)
    grad_value = heads_first(grad_value).reshape(length, -1)
    grads_out = ADAPTER_SCALE * jnp.stack([jnp.dot(low_query.T, grad_query, precision=HIGHEST), jnp.dot(low_value.T, grad_value, precision=HIGHEST)])
    grads_in = ADAPTER_SCALE * jnp.stack([jnp.dot(full_rows.T, jnp.dot(grad_query, adapter_out[0].T, precision=HIGHEST), precision=HIGHEST), jnp.dot(full_rows.T, jnp.dot(grad_value, adapter_out[1].T, precision=HIGHEST), precision=HIGHEST)])
    return (grads_in, grads_out)

def reference(frames, frame_counts, encoder_gain, encoder_shift, encoder_qkv, encoder_out, post_gain, post_shift, projector, projector_shift, text_embed, decoder_gain, decoder_qkv, adapter_in, adapter_out, audio_upstream, text_upstream):

    def one_clip(members):
        frames_clip, frame_count, text_rows, audio_grad, text_grad = members
        normed_frames = layer_norm(frames_clip, encoder_gain, encoder_shift).astype(jnp.bfloat16)
        queries = jnp.dot(normed_frames, encoder_qkv[0], preferred_element_type=jnp.float32).astype(jnp.bfloat16)
        keys_in = jnp.dot(normed_frames, encoder_qkv[1], preferred_element_type=jnp.float32).astype(jnp.bfloat16)
        values_in = jnp.dot(normed_frames, encoder_qkv[2], preferred_element_type=jnp.float32).astype(jnp.bfloat16)
        position = jnp.arange(frames_clip.shape[0], dtype=jnp.int32)
        context = encoder_attention(queries, keys_in, values_in, position < frame_count, EHD)
        hidden = frames_clip.astype(jnp.float32) + jnp.dot(context, encoder_out, preferred_element_type=jnp.float32)
        pooled = lax.optimization_barrier(jnp.mean(hidden.reshape(-1, 2, hidden.shape[1]), 1))
        pooled_norm = layer_norm(pooled, post_gain, post_shift).astype(jnp.bfloat16)
        embedded = (jnp.dot(pooled_norm, projector, preferred_element_type=jnp.float32) + projector_shift).astype(jnp.bfloat16)
        sequence = jnp.concatenate([embedded, text_rows], 0)
        normed = root_norm(sequence, decoder_gain)
        query_base = jnp.dot(normed, decoder_qkv[0], preferred_element_type=jnp.float32)
        key_base = jnp.dot(normed, decoder_qkv[1], preferred_element_type=jnp.float32)
        value_base = jnp.dot(normed, decoder_qkv[2], preferred_element_type=jnp.float32)
        upstream = jnp.concatenate([audio_grad, text_grad], 0)
        return adapter_grads(normed, query_base, key_base, value_base, upstream, frame_count, embedded.shape[0], adapter_in, adapter_out, HD)
    grads_in, grads_out = lax.map(one_clip, (frames, frame_counts, text_embed, audio_upstream, text_upstream))
    return (lax.optimization_barrier(jnp.sum(grads_in, 0)), lax.optimization_barrier(jnp.sum(grads_out, 0)))
```

```python
import math

import jax
import jax.numpy as jnp
from jax import lax
from jax.experimental import pallas as pl
from jax.experimental.pallas import tpu as pltpu
from jax.sharding import Mesh, PartitionSpec as P

BF = jnp.bfloat16
F32 = jnp.float32
I32 = jnp.int32
EPS_LAYER = 1e-05
EPS_ROOT = 1e-06
ROPE_BASE = 10000.0
LOG2E = math.log2(math.e)
MASKED = -1e30

ROWS = 750
POOL = 375
PADDED = 384
TEXT = 42
SEQ = 2 * PADDED + 48
KEYS = 2 * PADDED + 128
HEADS = 4
SWAP = ((0, 1), (1, 0))
QUAD = ("x", "y", "zl")


def dot(a, b):
    return jnp.dot(a, b, preferred_element_type=F32)


def dot_nt(a, b):
    return lax.dot_general(a, b, (((1,), (1,)), ((), ())), preferred_element_type=F32)


def dot_tn(a, b):
    return lax.dot_general(a, b, (((0,), (0,)), ((), ())), preferred_element_type=F32)


def layer_norm(values, gain, shift):
    values = values.astype(F32)
    center = values - jnp.mean(values, -1, keepdims=True)
    spread = jnp.mean(center * center, -1, keepdims=True)
    return center * lax.rsqrt(spread + EPS_LAYER) * gain + shift


def pool_matrix(columns):
    row = lax.broadcasted_iota(I32, (PADDED, columns), 0)
    column = lax.broadcasted_iota(I32, (PADDED, columns), 1)
    return jnp.where((column // 2) == row, 0.5, 0.0).astype(BF)


def encoder_kernel(info, q_ref, k_ref, v_ref, out_ref, qx, kx, vx, cx):
    head = pl.program_id(0)
    side = head % 2
    span = 2 * PADDED

    @pl.when(side == 0)
    def _():
        lane = lax.broadcasted_iota(I32, (span, 128), 1)
        row = lax.broadcasted_iota(I32, (span, 128), 0)
        for s in range(2):
            at = s * span
            place = (info[1] ^ s) * ROWS + row
            usable = (row < ROWS) & (place < info[0])
            tail = jnp.zeros((32, 128), BF)
            kx[at + span - 32 : at + span, :128] = tail
            vx[at + span - 32 : at + span, :128] = tail
            kx[at : at + ROWS, :128] = k_ref[s]
            vx[at : at + ROWS, :128] = v_ref[s]
            kx[at : at + span, 128:] = jnp.where((lane == 0) & ~usable, MASKED, 0.0).astype(BF)
            vx[at : at + span, 128:] = jnp.ones((span, 128), BF)
        cx[...] = jnp.zeros_like(cx)
        qx[:, 128:] = jnp.ones((2 * span, 128), BF)

    for s in range(2):
        at = s * span
        lane = lax.broadcasted_iota(I32, (ROWS, 128), 1)
        qx[at + span - 32 : at + span, :128] = jnp.zeros((32, 128), BF)
        qx[at : at + ROWS, :128] = jnp.where((lane // 64) == side, q_ref[s], jnp.zeros((), BF))
    mine = (lax.broadcasted_iota(I32, (256, 128), 1) // 64) == side
    for block in range(2 * span // 256):
        at = block * 256
        scores = dot_nt(qx[at : at + 256], kx[...])
        top = jnp.max(scores, -1, keepdims=True)
        weights = jnp.exp2(scores - top).astype(BF)
        total = dot(weights, vx[...])
        context = (total[:, :128] / total[:, 128:]).astype(BF)
        cx[at : at + 256] = jnp.where(mine, context, cx[at : at + 256])
    pool = pool_matrix(span)
    for s in range(2):
        out_ref[s] = dot(pool, cx[s * span : (s + 1) * span]).astype(BF)


def encoder_attention(info, qkv):
    grid_spec = pltpu.PrefetchScalarGridSpec(
        num_scalar_prefetch=1,
        grid=(5,),
        in_specs=[
            pl.BlockSpec((2, ROWS, 128), lambda h, info: (0, 0, h // 2)),
            pl.BlockSpec((2, ROWS, 128), lambda h, info: (0, 0, 3 + h // 2)),
            pl.BlockSpec((2, ROWS, 128), lambda h, info: (0, 0, 6 + h // 2)),
        ],
        out_specs=pl.BlockSpec((2, PADDED, 128), lambda h, info: (0, 0, h // 2)),
        scratch_shapes=[
            pltpu.VMEM((4 * PADDED, 256), BF),
            pltpu.VMEM((4 * PADDED, 256), BF),
            pltpu.VMEM((4 * PADDED, 256), BF),
            pltpu.VMEM((4 * PADDED, 128), BF),
        ],
    )
    return pl.pallas_call(
        encoder_kernel,
        grid_spec=grid_spec,
        out_shape=jax.ShapeDtypeStruct((2, PADDED, 384), BF),
        compiler_params=pltpu.CompilerParams(vmem_limit_bytes=40 * 2**20),
        name="encoder_attention",
    )(info, qkv, qkv, qkv)


BLOCKS = ((0, 192, 0, 256), (192, 192, 128, 384), (384, 192, 384, 640), (576, 192, 512, 768), (768, 48, 768, 896))


def decoder_kernel(info, normed, low, w_ref, aout, up, cosine, sine, gout, t_ref, qx, kx, vx, gq, gv):
    step = pl.program_id(0)

    @pl.when(step == 0)
    def _():
        row = lax.broadcasted_iota(I32, (KEYS, 128), 0)
        lane = lax.broadcasted_iota(I32, (KEYS, 128), 1)
        place = jnp.where(row < PADDED, row, row - (PADDED - POOL))
        real = (row < POOL) | ((row >= PADDED) & (row < PADDED + POOL))
        text = (row >= 2 * PADDED) & (row < 2 * PADDED + TEXT)
        usable = (real & (place < info[0])) | text
        kx[:, 128:] = jnp.where((lane == 0) & ~usable, MASKED, 0.0).astype(BF)
        kx[SEQ:, :128] = jnp.zeros((KEYS - SEQ, 128), BF)
        vx[SEQ:, :] = jnp.zeros((KEYS - SEQ, 128), BF)
        qx[:, 128:] = jnp.ones((SEQ, 128), BF)
        t_ref[...] = jnp.zeros_like(t_ref)

    base = dot(normed[...], w_ref[...])
    added = dot(low[...], aout[...])
    cos, sin = cosine[...], sine[...]

    def rope(x):
        return x * cos + pltpu.roll(x, 64, 1) * sin

    qx[:, :128] = (rope(base[:, :128] + added[:, :128]) * (LOG2E * 128**-0.5)).astype(BF)
    kx[:SEQ, :128] = rope(base[:, 128:256]).astype(BF)
    vx[:SEQ, :] = (base[:, 256:] + added[:, 128:]).astype(BF)
    gv[...] = jnp.zeros_like(gv)
    for r0, rows, cut, keys in BLOCKS:
        scores = dot_nt(qx[r0 : r0 + rows], kx[:keys])
        row = r0 + lax.broadcasted_iota(I32, (rows, keys - cut), 0)
        column = cut + lax.broadcasted_iota(I32, (rows, keys - cut), 1)
        diagonal = jnp.where(column <= row, scores[:, cut:], MASKED)
        scores = diagonal if cut == 0 else jnp.concatenate([scores[:, :cut], diagonal], 1)
        top = jnp.max(scores, -1, keepdims=True)
        weights = jnp.exp2(scores - top)
        probs = weights * (1.0 / jnp.sum(weights, -1, keepdims=True))
        rounded = probs.astype(BF)
        upstream = up[r0 : r0 + rows]
        context = dot(rounded, vx[:keys]).astype(BF)
        delta = jnp.sum(upstream.astype(F32) * context.astype(F32), -1, keepdims=True)
        grad_probs = dot_nt(upstream, vx[:keys])
        grad_scores = (probs * (grad_probs - delta)).astype(BF)
        gq[r0 : r0 + rows] = dot(grad_scores, kx[:keys, :128])
        gv[:keys] += dot_tn(rounded, upstream)
    g = gq[...]
    g = (g * cos + pltpu.roll(g * sin, 64, 1)) * (2.0 * 128**-0.5)
    both = jnp.concatenate([g.astype(BF), (2.0 * gv[:SEQ]).astype(BF)], 1)
    outer = dot_tn(low[...], both)
    gout[0, 0] = outer[:64, :128]
    gout[0, 1] = outer[64:, 128:]
    t_ref[...] += dot_nt(both, aout[...])


def decoder_heads(info, normed, low, weights, aout, up, cosine, sine):
    whole = lambda shape: pl.BlockSpec(shape, lambda h, info: (0, 0))
    grid_spec = pltpu.PrefetchScalarGridSpec(
        num_scalar_prefetch=1,
        grid=(HEADS,),
        in_specs=[
            whole((SEQ, 2048)),
            whole((SEQ, 128)),
            pl.BlockSpec((2048, 384), lambda h, info: (0, h)),
            pl.BlockSpec((128, 256), lambda h, info: (0, info[1] * HEADS + h)),
            pl.BlockSpec((SEQ, 128), lambda h, info: (0, info[1] * HEADS + h)),
            whole((SEQ, 128)),
            whole((SEQ, 128)),
        ],
        out_specs=[
            pl.BlockSpec((1, 2, 64, 128), lambda h, info: (h, 0, 0, 0)),
            whole((SEQ, 128)),
        ],
        scratch_shapes=[
            pltpu.VMEM((SEQ, 256), BF),
            pltpu.VMEM((KEYS, 256), BF),
            pltpu.VMEM((KEYS, 128), BF),
            pltpu.VMEM((SEQ, 128), F32),
            pltpu.VMEM((KEYS, 128), F32),
        ],
    )
    return pl.pallas_call(
        decoder_kernel,
        grid_spec=grid_spec,
        out_shape=[
            jax.ShapeDtypeStruct((HEADS, 2, 64, 128), F32),
            jax.ShapeDtypeStruct((SEQ, 128), F32),
        ],
        compiler_params=pltpu.CompilerParams(vmem_limit_bytes=48 * 2**20),
        name="decoder_heads",
    )(info, normed, low, weights, aout, up, cosine, sine)


def ordered(flag, mine, other, axis=0):
    return jnp.where(
        flag == 0, jnp.concatenate([mine, other], axis), jnp.concatenate([other, mine], axis)
    )


def rope_tables():
    row = jnp.arange(SEQ, dtype=I32)
    place = jnp.where(row < PADDED, row, row - (PADDED - POOL))
    place = jnp.where(row < 2 * PADDED, place, row - 2 * (PADDED - POOL)).astype(F32)
    frequency = ROPE_BASE ** (-jnp.arange(0, 128, 2).astype(F32) / 128)
    angles = place[:, None] * frequency[None, :]
    cos, sin = jnp.cos(angles), jnp.sin(angles)
    return jnp.concatenate([cos, cos], -1), jnp.concatenate([-sin, sin], -1)


def sections(audio, text):
    gap = lambda n: jnp.zeros((n, audio.shape[1]), audio.dtype)
    short = PADDED - POOL
    return jnp.concatenate([audio[:POOL], gap(short), audio[POOL:], gap(short), text, gap(6)], 0)


def per_device(
    frames,
    frame_counts,
    encoder_gain,
    encoder_shift,
    encoder_qkv,
    encoder_out,
    post_gain,
    post_shift,
    projector,
    projector_shift,
    text_embed,
    decoder_gain,
    decoder_qkv,
    adapter_in,
    adapter_out,
    audio_upstream,
    text_upstream,
):
    core, zl, tensor = lax.axis_index("core"), lax.axis_index("zl"), lax.axis_index("tensor")
    count = frame_counts[0]
    permute = lambda x, axis: lax.ppermute(x, axis, SWAP)

    a_shard = encoder_qkv.transpose(1, 0, 2).reshape(20, 960)
    a_shard = jnp.pad(a_shard, ((0, 0), (0, 64)))
    b_shard = jnp.concatenate([encoder_out.T, projector], 1)
    c_shard = decoder_qkv.reshape(3, 32, 8, 128).transpose(1, 2, 0, 3).reshape(32, 3072)

    def pick(shard, which):
        half = shard.shape[1] // 2
        return jnp.where(which == 0, shard[:, :half], shard[:, half:])

    a_quad = ordered(core, pick(a_shard, core), permute(pick(a_shard, 1 - core), "core"))
    a_quad = ordered(zl, a_quad, permute(a_quad, "zl"))
    c_quad = ordered(core, pick(c_shard, core), permute(pick(c_shard, 1 - core), "core"))
    c_quad = ordered(zl, c_quad, permute(c_quad, "zl"))
    b_quad = ordered(core, b_shard, permute(b_shard, "core"))
    b_other = lax.ppermute(b_quad, ("core", "tensor"), ((0, 1), (3, 2)))
    b_quad = jnp.where(core == tensor, b_quad, b_other)
    b_quad = ordered(zl, b_quad, permute(b_quad, "zl"))
    frames_mine = frames[0]
    frames_other = permute(frames_mine, "tensor")
    text_mine = text_embed[0]
    text_other = permute(text_mine, "tensor")

    b_half = lax.all_gather(b_quad, ("x", "y"), axis=0, tiled=True)
    c_half = lax.all_gather(c_quad, ("x", "y"), axis=0, tiled=True)
    a_half = lax.all_to_all(
        jnp.broadcast_to(a_quad[None], (16, 80, 512)), ("x", "y"), split_axis=0, concat_axis=0, tiled=True
    ).reshape(1280, 512)
    a_all = ordered(core, a_half, permute(a_half, "core"), 1)
    zeros = jnp.zeros((1280, 64), BF)
    a_all = jnp.concatenate([a_all[:, :320], zeros, a_all[:, 320:640], zeros, a_all[:, 640:960], zeros], 1)

    column_scale = jnp.where(jnp.arange(1152) < 384, LOG2E * 64**-0.5, 1.0).astype(F32)

    def project(rows):
        normed = layer_norm(rows, encoder_gain, encoder_shift).astype(BF)
        return (dot(normed, a_all) * column_scale).astype(BF)

    qkv = jnp.stack([project(frames_mine), project(frames_other)])
    info = jnp.stack([count, tensor]).astype(I32)
    context = encoder_attention(info, qkv)
    context_other = permute(context, "tensor")
    pool = pool_matrix(ROWS)
    pooled_frames = jnp.stack([dot(pool, frames_mine), dot(pool, frames_other)])

    b_other_half = permute(b_half, "core")
    out_t = [jnp.where(core == i, b_half[:, :320], b_other_half[:, :320]) for i in range(2)]
    proj = jnp.concatenate(
        [jnp.where(core == i, b_half[:, 320:], b_other_half[:, 320:]) for i in range(2)], 1
    )
    out_mine = jnp.where(tensor == 0, out_t[0], out_t[1])
    out_other = jnp.where(tensor == 0, out_t[1], out_t[0])
    flat = lambda x: x.reshape(2 * PADDED, -1)
    attended = dot_nt(flat(context)[:, :320], out_mine) + dot_nt(
        flat(context_other[::-1])[:, :320], out_other
    )
    pooled = flat(pooled_frames) + attended
    pooled_norm = layer_norm(pooled, post_gain, post_shift).astype(BF)
    embedded = (dot(pooled_norm, proj) + projector_shift).astype(BF)
    embedded = jnp.where(tensor == 0, embedded, jnp.concatenate([embedded[PADDED:], embedded[:PADDED]], 0))
    text = ordered(tensor, text_mine, text_other)
    sequence = jnp.concatenate([embedded, text, jnp.zeros((6, 2048), BF)], 0).astype(F32)
    row = jnp.arange(SEQ)
    real = (row < POOL) | ((row >= PADDED) & (row < PADDED + POOL)) | (row >= 2 * PADDED)
    normed = (
        sequence * lax.rsqrt(jnp.mean(sequence * sequence, -1, keepdims=True) + EPS_ROOT) * decoder_gain
    ).astype(BF)
    normed = jnp.where(real[:, None], normed, jnp.zeros((), BF))

    rank = jnp.arange(64)
    spread = ((rank % 2) * 32 + rank // 2)[:, None] == rank[None, :]
    spread = spread.astype(F32)
    down = jnp.concatenate([adapter_in[0] @ spread, adapter_in[1] @ spread], 1).astype(BF)
    up_maps = [(spread.T @ adapter_out[i]).reshape(64, 8, 128) for i in range(2)]
    nothing = jnp.zeros((64, 8, 128), F32)
    aout = jnp.concatenate(
        [
            jnp.stack([2.0 * up_maps[0], nothing], 2).reshape(64, 2048),
            jnp.stack([nothing, 2.0 * up_maps[1]], 2).reshape(64, 2048),
        ],
        0,
    ).astype(BF)
    low = dot(normed, down).astype(BF)
    upstream = sections(audio_upstream[0], text_upstream[0])
    cosine, sine = rope_tables()
    limit = (count + 1) // 2
    c_other = permute(c_half, "core")
    gout_a, t_a = decoder_heads(jnp.stack([limit, core]).astype(I32), normed, low, c_half, aout, upstream, cosine, sine)
    gout_b, t_b = decoder_heads(jnp.stack([limit, 1 - core]).astype(I32), normed, low, c_other, aout, upstream, cosine, sine)
    gout = ordered(core, gout_a, gout_b)
    t_all = ((t_a + t_b) * 0.5).astype(BF)
    gin = dot_tn(normed, t_all)

    gin = gin.reshape(32, 2, 32, 128)
    gout = gout.transpose(1, 2, 0, 3).reshape(2, 2, 32, 1024).transpose(1, 2, 0, 3).reshape(2, 32, 16, 128)
    both = jnp.concatenate([gin.transpose(1, 0, 2, 3), gout], 2)
    away = jnp.where(core == 0, both[1], both[0]).astype(BF)
    kept = jnp.where(core == 0, both[0], both[1])
    kept = (kept + permute(away, "core").astype(F32)).astype(BF)
    kept = lax.all_to_all(kept, QUAD, split_axis=0, concat_axis=0, tiled=True)
    total = jnp.sum(kept.astype(F32), 0)
    give = jnp.where(tensor == 0, total[16:32], total[:16])
    own = jnp.where(tensor == 0, total[:16], total[16:32])
    own = own + permute(give, "tensor")
    grads_in = own.reshape(16, 2, 2, 32).transpose(1, 0, 3, 2).reshape(2, 16, 64)
    grads_out = total[32:].reshape(2, 1, 1024)
    return grads_in, grads_out


def solution(mesh):
    fine = Mesh(mesh.devices.reshape(4, 4, 2, 2, 2), ("x", "y", "zl", "core", "tensor"))
    dp = ("x", "y", "zl", "core")
    in_specs = (
        P(dp, "tensor", None),
        P(dp),
        P(),
        P(),
        P(None, dp, "tensor"),
        P("tensor", dp),
        P(),
        P(),
        P(dp, "tensor"),
        P(),
        P(dp, "tensor", None),
        P(),
        P(None, dp, "tensor"),
        P(),
        P(None, None, "tensor"),
        P(dp, None, "tensor"),
        P(dp, None, "tensor"),
    )
    out_specs = (P(None, (*dp, "tensor"), None), P(None, dp, "tensor"))
    return jax.shard_map(
        per_device, mesh=fine, in_specs=in_specs, out_specs=out_specs, check_vma=False
    )
```
